32 devices in a mesh: dp: 4 (over x, core), seq: 8 (over z, y).
Axes of the slice: x: 2, y: 2, z: 4, core: 2. Of those that a mesh axis runs over, the one named last changes fastest.
Arguments:
- signal: float32 [32, 512, 1024], P('seq', None, 'dp'), may hold values from -6 to 6
- gate: float32 [32, 512, 1024], P('seq', None, 'dp'), may hold values from -6 to 6
- cotangent: float32 [32, 512, 1024], P('seq', None, 'dp'), may hold values from -6 to 6
- kernel: float32 [2, 32, 512, 1024], P(None, 'seq', None, 'dp'), may hold values from -6 to 6
- out_weight: float32 [1024, 1024], P('dp'), may hold values from -0.1875 to 0.1875
Outputs:
- output: float32 [32, 512, 1024], P('seq', None, 'dp')
- gate_grad: float32 [32, 512, 1024], P('seq', None, 'dp')
- input_grad: float32 [32, 512, 1024], P('seq', None, 'dp')
- kernel_grad: float32 [2, 32, 512, 1024], P(None, 'seq', None, 'dp')
- weight_grad: float32 [1024, 1024], P('dp')
The draws below stay inside these ranges and needn't reach their ends.
All inputs are finite; a program needn't handle non-finite values.
Results may differ from the reference program's by a relative error of at most 0.000098.
Values sent between devices are 32-bit elements; how exact they have to be, the bound alone decides.
A program may use at most 128 MiB of HBM per device.

```python
import jax
import jax.numpy as jnp
from jax import lax

N1 = 32
N2 = 512
CH = 1024


def levels(rng, shape, pieces, smallest, top_value):
    factor_of = 1.0
    for position, parts in pieces:
        steps = jax.random.uniform(jax.random.fold_in(jax.random.fold_in(rng, 6), position), (parts,), jnp.float32, smallest / len(pieces), top_value / len(pieces))
        factor_of = factor_of * jnp.repeat(jnp.exp(steps), shape[position] // parts).reshape((-1,) + (1,) * (len(shape) - 1 - position))
    return factor_of


def gaussian(key, extent, spread, most, pieces=(), kind=jnp.bfloat16):
    result = spread * jax.random.normal(key, extent, jnp.float32)
    if pieces:
        result = result * levels(key, extent, pieces, -0.22, 0.18)
    return jnp.clip(result, -most, most).astype(kind)


def setup_inputs(seed: int = 0) -> dict:
    splits = jax.random.split(jax.random.key(seed), 6)
    return {
        "signal": gaussian(splits[0], (N1, N2, CH), 1.0, 6.0, ((0, 8), (2, 4)), jnp.float32),
        "gate": gaussian(splits[1], (N1, N2, CH), 1.0, 6.0, ((0, 8), (2, 4)), jnp.float32),
        "cotangent": gaussian(splits[2], (N1, N2, CH), 1.0, 6.0, ((0, 8), (2, 4)), jnp.float32),
        "kernel": gaussian(splits[3], (2, N1, N2, CH), 1.0, 6.0, ((1, 8), (3, 4)), jnp.float32),
        "out_weight": gaussian(splits[4], (CH, CH), CH ** -0.5, 0.1875, ((0, 4),), jnp.float32),
    }


PRECISE = lax.Precision.HIGHEST


def spectrum(field):
    flat = field.reshape(N1 * N2, CH)
    freq = jnp.fft.fft(flat, axis=0).reshape(N2, N1, CH)
    freq = jnp.transpose(freq, (1, 0, 2))
    return jnp.real(freq), jnp.imag(freq)


def restore(real_part, imag_part):
    freq = jnp.transpose(real_part + 1j * imag_part, (1, 0, 2)).reshape(N1 * N2, CH)
    return jnp.real(jnp.fft.ifft(freq, axis=0)).reshape(N1, N2, CH)


def reference(signal, gate, cotangent, kernel, out_weight):
    kern_re = kernel[0]
    kern_im = kernel[1]
    signal_re, signal_im = spectrum(signal)
    mixed = restore(kern_re * signal_re - kern_im * signal_im, kern_re * signal_im + kern_im * signal_re)
    gated = gate * mixed
    output = jnp.einsum("abc,co->abo", gated, out_weight, precision=PRECISE)
    gated_grad = jnp.einsum("abo,co->abc", cotangent, out_weight, precision=PRECISE)
    weight_grad = jnp.einsum("abc,abo->co", gated, cotangent, precision=PRECISE)
    gate_grad = gated_grad * mixed
    conv_grad = gated_grad * gate
    grad_re, grad_im = spectrum(conv_grad)
    input_grad = restore(kern_re * grad_re + kern_im * grad_im, kern_re * grad_im - kern_im * grad_re)
    partial_re = signal_re * grad_re + signal_im * grad_im
    partial_im = signal_re * grad_im - signal_im * grad_re
    kernel_grad = jnp.stack([partial_re, partial_im]) / (N1 * N2)
    return output, gate_grad, input_grad, kernel_grad, weight_grad
```

```python
import jax
import jax.numpy as jnp
import numpy as np
from jax import lax
from jax.sharding import PartitionSpec as P

PRECISE = lax.Precision.HIGH


def dft(n):
    index = np.arange(n, dtype=np.int64)
    angle = (index[:, None] * index[None, :] % n) * (2.0 * np.pi / n)
    return np.cos(angle).astype(np.float32), np.sin(angle).astype(np.float32)


def twiddle(n1, n2):
    index = np.arange(n1, dtype=np.int64)[:, None] * np.arange(n2, dtype=np.int64)[None, :]
    angle = (index % (n1 * n2)) * (2.0 * np.pi / (n1 * n2))
    shape = (n1, 1, n2)
    return (
        np.cos(angle).astype(np.float32).reshape(shape),
        np.sin(angle).astype(np.float32).reshape(shape),
    )


def contract(form, left, right):
    return jnp.einsum(form, left, right, precision=PRECISE)


def to_channels(field):
    devices = lax.axis_size("seq")
    rows, cols, channels = field.shape
    share = channels // devices
    blocks = field.reshape(rows, cols, devices, share).transpose(2, 0, 3, 1)
    moved = lax.all_to_all(blocks, "seq", split_axis=0, concat_axis=0, tiled=True)
    return moved.reshape(devices * rows, share, cols)


def to_rows(field):
    devices = lax.axis_size("seq")
    all_rows, share, cols = field.shape
    rows = all_rows // devices
    blocks = field.reshape(devices, rows, share, cols)
    moved = lax.all_to_all(blocks, "seq", split_axis=0, concat_axis=0, tiled=True)
    return moved.transpose(1, 3, 0, 2).reshape(rows, cols, devices * share)


def forward(field):
    n1, _, n2 = field.shape
    cos1, sin1 = dft(n1)
    cos2, sin2 = dft(n2)
    tcos, tsin = twiddle(n1, n2)
    re = contract("ka,acb->kcb", cos1, field)
    im = -contract("ka,acb->kcb", sin1, field)
    tre = re * tcos + im * tsin
    tim = im * tcos - re * tsin
    return (
        contract("kcb,bm->kcm", tre, cos2) + contract("kcb,bm->kcm", tim, sin2),
        contract("kcb,bm->kcm", tim, cos2) - contract("kcb,bm->kcm", tre, sin2),
    )


def inverse(re, im):
    n1, _, n2 = re.shape
    cos1, sin1 = dft(n1)
    cos2, sin2 = dft(n2)
    tcos, tsin = twiddle(n1, n2)
    hre = contract("kcm,mb->kcb", re, cos2) - contract("kcm,mb->kcb", im, sin2)
    him = contract("kcm,mb->kcb", im, cos2) + contract("kcm,mb->kcb", re, sin2)
    tre = hre * tcos - him * tsin
    tim = him * tcos + hre * tsin
    scale = np.float32(1.0 / (n1 * n2))
    return contract("ak,kcb->acb", cos1 * scale, tre) - contract("ak,kcb->acb", sin1 * scale, tim)


def on_device(signal, gate, cotangent, kernel, out_weight):
    sig = to_channels(signal)
    kern_re = to_channels(kernel[0])
    kern_im = to_channels(kernel[1])

    cot_full = lax.all_gather(cotangent, "dp", axis=2, tiled=True)
    gated_grad = contract("abo,co->abc", cot_full, out_weight)
    conv = to_channels(gated_grad * gate)

    sre, sim = forward(sig)
    mixed = to_rows(inverse(kern_re * sre - kern_im * sim, kern_re * sim + kern_im * sre))

    gre, gim = forward(conv)
    size = np.float32(1.0 / (gre.shape[0] * gre.shape[2]))
    kgrad_re = to_rows((sre * gre + sim * gim) * size)
    kgrad_im = to_rows((sre * gim - sim * gre) * size)
    input_grad = to_rows(inverse(kern_re * gre + kern_im * gim, kern_re * gim - kern_im * gre))

    gated = gate * mixed
    gate_grad = gated_grad * mixed
    out_term = contract("abc,co->abo", gated, out_weight)
    output = lax.psum_scatter(out_term, "dp", scatter_dimension=2, tiled=True)
    weight_grad = lax.psum(contract("abc,abo->co", gated, cot_full), "seq")
    return output, gate_grad, input_grad, jnp.stack([kgrad_re, kgrad_im]), weight_grad


def solution(mesh):
    grid = P("seq", None, "dp")
    spectrum = P(None, "seq", None, "dp")
    weight = P("dp", None)
    return jax.shard_map(
        on_device,
        mesh=mesh,
        in_specs=(grid, grid, grid, spectrum, weight),
        out_specs=(grid, grid, grid, spectrum, weight),
        check_vma=False,
    )
```

```python
import jax
import jax.numpy as jnp
import numpy as np
from jax import lax
from jax.sharding import PartitionSpec as P

PRECISE = lax.Precision.HIGH


def dft(n):
    index = np.arange(n, dtype=np.int64)
    angle = (index[:, None] * index[None, :] % n) * (2.0 * np.pi / n)
    return np.cos(angle).astype(np.float32), np.sin(angle).astype(np.float32)


def twiddle(n1, n2):
    index = np.arange(n1, dtype=np.int64)[:, None] * np.arange(n2, dtype=np.int64)[None, :]
    angle = (index % (n1 * n2)) * (2.0 * np.pi / (n1 * n2))
    shape = (n1, 1, n2)
    return (
        np.cos(angle).astype(np.float32).reshape(shape),
        np.sin(angle).astype(np.float32).reshape(shape),
    )


def contract(form, left, right):
    return jnp.einsum(form, left, right, precision=PRECISE)


def exchange(blocks):
    return lax.all_to_all(blocks, "seq", split_axis=0, concat_axis=0, tiled=True)


def after(value, *earlier):
    return lax.optimization_barrier((value, *earlier))[0]


def to_blocks(field):
    devices = lax.axis_size("seq")
    *lead, rows, cols, channels = field.shape
    blocks = field.reshape(*lead, rows, cols, devices, channels // devices)
    n = len(lead)
    return blocks.transpose(n + 2, *range(n), n, n + 3, n + 1)


def from_blocks(blocks):
    devices, *lead, rows, share, cols = blocks.shape
    n = len(lead)
    field = blocks.transpose(*range(1, n + 1), n + 1, n + 3, 0, n + 2)
    return field.reshape(*lead, rows, cols, devices * share)


def join(blocks):
    return blocks.reshape(-1, *blocks.shape[2:])


def part(field):
    return field.reshape(lax.axis_size("seq"), -1, *field.shape[1:])


def forward(field):
    n1, _, n2 = field.shape
    cos1, sin1 = dft(n1)
    cos2, sin2 = dft(n2)
    tcos, tsin = twiddle(n1, n2)
    re = contract("ka,acb->kcb", cos1, field)
    im = -contract("ka,acb->kcb", sin1, field)
    tre = re * tcos + im * tsin
    tim = im * tcos - re * tsin
    return (
        contract("kcb,bm->kcm", tre, cos2) + contract("kcb,bm->kcm", tim, sin2),
        contract("kcb,bm->kcm", tim, cos2) - contract("kcb,bm->kcm", tre, sin2),
    )


def inverse(re, im):
    n1, _, n2 = re.shape
    cos1, sin1 = dft(n1)
    cos2, sin2 = dft(n2)
    tcos, tsin = twiddle(n1, n2)
    hre = contract("kcm,mb->kcb", re, cos2) - contract("kcm,mb->kcb", im, sin2)
    him = contract("kcm,mb->kcb", im, cos2) + contract("kcm,mb->kcb", re, sin2)
    tre = hre * tcos - him * tsin
    tim = him * tcos + hre * tsin
    scale = np.float32(1.0 / (n1 * n2))
    return contract("ak,kcb->acb", cos1 * scale, tre) - contract("ak,kcb->acb", sin1 * scale, tim)


def on_device(signal, gate, cotangent, kernel, out_weight):
    cot_full = lax.all_gather(cotangent, "dp", axis=2, tiled=True)

    sig = exchange(to_blocks(signal))
    kern = exchange(after(to_blocks(kernel), sig))
    gated_grad = contract("abo,co->abc", cot_full, out_weight)
    conv = exchange(after(to_blocks(gated_grad * gate), kern))
    kern_re, kern_im = join(kern[:, 0]), join(kern[:, 1])

    sre, sim = lax.optimization_barrier(forward(join(sig)))
    mixed = inverse(kern_re * sre - kern_im * sim, kern_re * sim + kern_im * sre)
    mixed, conv = lax.optimization_barrier((part(mixed), conv))
    mixed = exchange(mixed)

    gre, gim = lax.optimization_barrier(forward(join(conv)))
    size = np.float32(1.0 / (gre.shape[0] * gre.shape[2]))
    kgrad_re = (sre * gre + sim * gim) * size
    kgrad_im = (sre * gim - sim * gre) * size
    kgrad = jnp.stack([part(kgrad_re), part(kgrad_im)], axis=1)
    kgrad, mixed = lax.optimization_barrier((kgrad, mixed))
    kgrad = exchange(kgrad)
    igrad = inverse(kern_re * gre + kern_im * gim, kern_re * gim - kern_im * gre)
    igrad = exchange(after(part(igrad), kgrad))

    mixed = from_blocks(mixed)
    gated = gate * mixed
    gate_grad = gated_grad * mixed
    out_term = contract("abc,co->abo", gated, out_weight)
    output = lax.psum_scatter(out_term, "dp", scatter_dimension=2, tiled=True)
    weight_grad = lax.psum(contract("abc,abo->co", gated, cot_full), "seq")
    return output, gate_grad, from_blocks(igrad), from_blocks(kgrad), weight_grad


def solution(mesh):
    grid = P("seq", None, "dp")
    spectrum = P(None, "seq", None, "dp")
    weight = P("dp", None)
    return jax.shard_map(
        on_device,
        mesh=mesh,
        in_specs=(grid, grid, grid, spectrum, weight),
        out_specs=(grid, grid, grid, spectrum, weight),
        check_vma=False,
    )
```
